32 devices in a mesh: parts: 2 (over y), node: 4 (over x, core), local: 4 (over z).
Axes of the slice: x: 2, y: 2, z: 4, core: 2. Of those that a mesh axis runs over, the one named last changes fastest.
Arguments:
- tokens: bfloat16 [4096, 3584], P(('parts', 'node', 'local')), parts along dimension 0, may hold values from -6 to 6
- expert_ids: int32 [4096, 3], P(('parts', 'node', 'local')), parts along dimension 0, may hold values from 0 to 15, all different within a row; in each aligned block of 128 rows (0 to 127, 128 to 255, ...) at most 32 rows name the same one
- gate_weights: float32 [4096, 3], P(('parts', 'node', 'local')), parts along dimension 0, may hold values from 0.1 to 1
- gate_proj: bfloat16 [16, 3584, 1024], P(('node', 'local')), may hold values from -0.09375 to 0.09375
- up_proj: bfloat16 [16, 3584, 1024], P(('node', 'local')), may hold values from -0.09375 to 0.09375
- down_proj: bfloat16 [16, 1024, 3584], P(('node', 'local')), may hold values from -0.1875 to 0.1875
Outputs:
- combined: bfloat16 [4096, 3584], P(('parts', 'node', 'local')), parts along dimension 0
The draws below stay inside these ranges and needn't reach their ends.
There are 2 independent parts, one for each index of `parts`. The reference program is written for one: setup_inputs(seed, part) draws one part's arguments, and reference() takes and returns one part's arrays. A program takes and returns all parts, laid end to end along the dimension named above; an argument that names none is the same for every part. Nothing has to cross between parts.
Inputs may be any that keep to these rules, and one draw needn't show every extreme that they name: `expert_ids`: each row names 3 different experts; among the rows of one device no expert is named by more than 32 rows, a bound that some block reaches.
All inputs are finite; a program needn't handle non-finite values.
Results may differ from the reference program's by a relative error of at most 0.0058.
Values may be sent and summed in bfloat16 or wider, within the bound.
A program may use at most 128 MiB of HBM per device.

```python
import math
import jax
import jax.numpy as jnp
import numpy as np
from jax import lax

D = 3584
FF = 1024
EPG = 4
TOPK = 3
TOK_DEV = 128
EXPERTS = 16
WSPLIT = 1
FF_DEV = 1024
CAP = 32
TOKENS = 2048
N_NODE = 4
N_LOCAL = 4


def level_of(stream_key, shape, cuts, smallest, high):
    def one(dim, blocks):
        steps = jax.random.uniform(jax.random.fold_in(jax.random.fold_in(stream_key, 6), dim), (blocks,), jnp.float32, smallest / len(cuts), high / len(cuts))
        return jnp.repeat(jnp.exp(steps), shape[dim] // blocks).reshape((-1,) + (1,) * (len(shape) - dim - 1))

    loudness = one(*cuts[0])
    for cut in cuts[1:]:
        loudness = loudness * one(*cut)
    return loudness


def routed_block(own_key, own, number, rows, count, top, most, lean):
    order = jax.random.permutation(own_key, count)
    crowded, ordinary = shares(count, rows * top, most, lean, True), shares(count, rows * top, most, lean, False)
    places = jnp.arange(count)

    def named(sizes, rotation):
        used = int((sizes > 0).sum())
        fixed = max(1, used // 4)
        passed = fixed + (places - fixed + rotation * (used - fixed)) % max(1, count - fixed)
        return jnp.zeros((count,), jnp.int32).at[order[jnp.where(places < fixed, places, passed)]].set(jnp.asarray(sizes, jnp.int32))

    sizes = jnp.where(number % 4 == 0, named(crowded, number // 4), named(ordinary, number - number // 4 - 1))
    mixed = jax.random.permutation(jax.random.fold_in(own, 3), count)
    giver, sink = mixed[0:count // 2 * 2:2], mixed[1:count // 2 * 2:2]
    room = jnp.minimum(sizes[giver] - 1, most - sizes[sink]) // 2
    room = jnp.where((giver == order[0]) | (sink == order[0]) | (sizes[sink] == 0), 0, jnp.maximum(room, 0))
    passed = jax.random.randint(jax.random.fold_in(own, 4), (count // 2,), 0, 1 << 20) % (room + 1)
    sizes = sizes.at[giver].add(-passed).at[sink].add(passed)
    members = jnp.searchsorted(jnp.cumsum(sizes), jnp.arange(rows * top), side="right").astype(jnp.int32)
    table = members.reshape(top, rows).T
    table = table[jax.random.permutation(jax.random.fold_in(own, 1), rows)]
    rotation = jax.random.randint(jax.random.fold_in(own, 2), (rows, 1), 0, top)
    return jnp.take_along_axis(table, (jnp.arange(top)[None, :] + rotation) % top, axis=1)


def shares(amount, total, bound, skew, full):
    loads = [(1 << 20) // math.isqrt(grade ** skew) + 1 for grade in range(1, amount + 1)]
    largest = bound if full else min(bound, max(-(-total // amount), total * loads[0] // sum(loads)))
    least = 1 if total - largest >= amount - 1 else 0
    counts, rest = [largest] + [least] * (amount - 1), total - largest - least * (amount - 1)
    while rest > 0:
        free = [i for i in range(1, amount) if counts[i] < largest] or [i for i in range(1, amount) if counts[i] < bound]
        pool, remaining = sum([loads[i] for i in free]), rest
        for i in free:
            addition = min(bound - counts[i], max(1, remaining * loads[i] // pool), rest)
            counts[i] = counts[i] + addition
            rest = rest - addition
    return np.array(counts)


def scatter_about(own_key, shape, deviation, most, shards=(), kind=jnp.bfloat16):
    result = jax.random.normal(own_key, shape, jnp.float32) * deviation
    if len(shards) > 0:
        result = level_of(own_key, shape, shards, -0.22, 0.18) * result
    return jnp.clip(result, min=-most, max=most).astype(kind)


def setup_inputs(seed: int = 0, part: int = 0) -> dict:
    keys = jax.random.split(jax.random.key(seed), 7)
    part_splits = jax.random.split(jax.random.fold_in(keys[6], part), 7)
    tokens = scatter_about(part_splits[0], (TOKENS, D), 1.0, 6.0, ((0, 16),))
    expert_ids_keys = jax.random.split(jax.random.fold_in(part_splits[1], 1), TOKENS // TOK_DEV)
    expert_ids_turns = jax.random.permutation(jax.random.fold_in(part_splits[1], 3), TOKENS // TOK_DEV)
    expert_ids = jax.vmap(lambda own, number: routed_block(jax.random.fold_in(part_splits[1], 2), own, number, TOK_DEV, EXPERTS, TOPK, CAP, 2))(expert_ids_keys, expert_ids_turns).reshape((TOKENS, TOPK))
    gate_weights = jnp.clip(jnp.exp(math.log(1.0) - 2.3025851 * jax.random.uniform(part_splits[2], (TOKENS, TOPK), jnp.float32) ** level_of(part_splits[2], (TOKENS, TOPK), ((0, 16),), -0.2, 0.2)), 0.1, 1.0)
    gate_proj = scatter_about(keys[3], (EXPERTS * WSPLIT, D, FF_DEV), D ** -0.5, 0.09375, ((0, 16),))
    up_proj = scatter_about(keys[4], (EXPERTS * WSPLIT, D, FF_DEV), D ** -0.5, 0.09375, ((0, 16),))
    down_proj = scatter_about(keys[5], (EXPERTS * WSPLIT, FF_DEV, D), FF ** -0.5, 0.1875, ((0, 16),))
    return dict(tokens=tokens, expert_ids=expert_ids, gate_weights=gate_weights, gate_proj=gate_proj, up_proj=up_proj, down_proj=down_proj)


def expert_rows(rows, gate_mat, up_mat, down_mat):
    gate_act = jnp.dot(rows, gate_mat, preferred_element_type=jnp.float32)
    up_act = jnp.dot(rows, up_mat, preferred_element_type=jnp.float32)
    hidden = (jax.nn.silu(gate_act) * up_act).astype(jnp.bfloat16)
    return jnp.dot(hidden, down_mat, preferred_element_type=jnp.float32).astype(jnp.bfloat16)


def reference(tokens, expert_ids, gate_weights, gate_proj, up_proj, down_proj):
    wsplit = N_LOCAL // EPG
    max_rows = N_NODE * N_LOCAL * CAP

    def visit(accumulated, inputs):
        gate_mat, up_mat, down_mat, shard_id = inputs
        expert = (shard_id // wsplit).astype(jnp.int32)
        matched = expert_ids == expert
        weight = jnp.sum(jnp.where(matched, gate_weights, jnp.zeros_like(gate_weights)), axis=1)
        chosen = jnp.any(matched, axis=1)
        positions = jnp.nonzero(chosen, size=max_rows, fill_value=0)[0].astype(jnp.int32)
        live_count = jnp.sum(chosen.astype(jnp.int32))
        is_live = jnp.arange(max_rows, dtype=jnp.int32) < live_count
        row_weight = jnp.where(is_live, weight[positions], jnp.zeros_like(weight[positions]))
        partial_value = expert_rows(tokens[positions], gate_mat, up_mat, down_mat)
        accumulated = accumulated.at[positions].add(partial_value.astype(jnp.float32) * row_weight[:, None])
        return accumulated, None

    shard_ids = jnp.arange(N_NODE * N_LOCAL, dtype=jnp.int32)
    start = jnp.zeros((TOKENS, D), jnp.float32)
    accumulated, unused = lax.scan(visit, start, (gate_proj, up_proj, down_proj, shard_ids))
    return accumulated.astype(jnp.bfloat16)
```

```python
import functools

import jax
import jax.numpy as jnp
from jax import lax
from jax.experimental import pallas as pl
from jax.experimental.pallas import tpu as pltpu
from jax.sharding import PartitionSpec as P

EPG = 4
CHUNKS = 4
VMEM_BUDGET = 60 * 1024 * 1024
MESH = pl.DeviceIdType.MESH


def routing(expert_ids, experts):
    matches = expert_ids[:, :, None] == jnp.arange(experts, dtype=jnp.int32)[None, None, :]
    chosen = jnp.sum(matches.astype(jnp.int32), axis=1)
    ranking = jnp.cumsum(chosen, axis=0) - chosen
    rank = jnp.sum(jnp.where(matches, ranking[:, None, :], 0), axis=2)
    return rank


def split_weight(weight):
    high = weight.astype(jnp.bfloat16)
    low = (weight - high.astype(jnp.float32)).astype(jnp.bfloat16)
    return high, low


def expert_rows(received, gate_mat, up_mat, down_mat):
    features = received.shape[-1]
    flattened = received.reshape(-1, features)
    gate_act = jnp.dot(flattened, gate_mat, preferred_element_type=jnp.float32)
    up_act = jnp.dot(flattened, up_mat, preferred_element_type=jnp.float32)
    hidden = (jax.nn.silu(gate_act) * up_act).astype(jnp.bfloat16)
    output = jnp.dot(hidden, down_mat, preferred_element_type=jnp.float32).astype(jnp.bfloat16)
    return output.reshape(received.shape)


def by_collectives(tokens, codes, gate_weights, gate_proj, up_proj, down_proj, experts, wsplit, capacity):
    tok_dev, features = tokens.shape
    slots = jnp.arange(experts * capacity, dtype=jnp.int32)
    hit = codes[:, :, None] == slots[None, None, :]
    selected = jnp.any(hit, axis=1).astype(jnp.bfloat16).T
    packed = jnp.dot(selected, tokens, preferred_element_type=jnp.float32).astype(jnp.bfloat16)
    packed = jnp.broadcast_to(
        packed.reshape(experts, 1, capacity, features), (experts, wsplit, capacity, features)
    ).reshape(experts * wsplit, capacity, features)
    outputs = expert_rows(
        lax.all_to_all(packed, ("node", "local"), split_axis=0, concat_axis=0, tiled=True),
        gate_proj[0], up_proj[0], down_proj[0],
    )
    returned = lax.all_to_all(outputs, ("node", "local"), split_axis=0, concat_axis=0, tiled=True)
    weight = jnp.sum(jnp.where(hit, gate_weights[:, :, None], 0.0), axis=1)
    weight = jnp.broadcast_to(
        weight.reshape(tok_dev, experts, 1, capacity), (tok_dev, experts, wsplit, capacity)
    ).reshape(tok_dev, -1)
    high, low = split_weight(weight)
    returned = returned.reshape(-1, features)
    combined = jnp.dot(high, returned, preferred_element_type=jnp.float32)
    combined = combined + jnp.dot(low, returned, preferred_element_type=jnp.float32)
    return combined.astype(jnp.bfloat16)


def kernel(
    nodes, planes, wsplit, capacity, topk,
    tok_ref, meta_ref, gate_hbm, up_hbm, down_hbm, out_ref,
    gath, metas, pack, recv, ret, inc, hid, wg, wu, wd,
    w_sem, g_send, g_recv, m_send, m_recv, p_send, p_recv, r_send, r_recv, i_send, i_recv,
):
    n = lax.axis_index("node")
    l = lax.axis_index("local")
    tok, features = tok_ref.shape
    ff = wg.shape[1]
    slots = nodes * capacity
    rows = tok // CHUNKS

    def other_node(d):
        return lax.rem(n + d, nodes)

    def other_plane(d):
        return lax.rem(l + d, planes)

    barrier = pltpu.get_barrier_semaphore()
    for d in range(1, nodes):
        pl.semaphore_signal(barrier, inc=1, device_id={"node": other_node(d)}, device_id_type=MESH)
    for d in range(1, planes):
        pl.semaphore_signal(barrier, inc=1, device_id={"local": other_plane(d)}, device_id_type=MESH)

    loads = [
        pltpu.make_async_copy(gate_hbm.at[0], wg, w_sem.at[0]),
        pltpu.make_async_copy(up_hbm.at[0], wu, w_sem.at[1]),
        pltpu.make_async_copy(down_hbm.at[0], wd, w_sem.at[2]),
    ]
    for load in loads:
        load.start()
    gath[l] = tok_ref[...]
    metas[l] = meta_ref[...]
    pl.semaphore_wait(barrier, nodes - 1 + planes - 1)

    def block_copy(src, way, plane):
        return pltpu.make_async_remote_copy(
            src_ref=gath.at[src], dst_ref=gath.at[src], send_sem=g_send.at[way, src], recv_sem=g_recv.at[src],
            device_id={"local": plane}, device_id_type=MESH,
        )

    def meta_copy(src, plane):
        return pltpu.make_async_remote_copy(
            src_ref=metas.at[src], dst_ref=metas.at[src], send_sem=m_send.at[plane], recv_sem=m_recv.at[src],
            device_id={"local": plane}, device_id_type=MESH,
        )

    def pack_copy(src, to, slot):
        return pltpu.make_async_remote_copy(
            src_ref=pack.at[src, to], dst_ref=recv.at[src, slot], send_sem=p_send.at[src, to], recv_sem=p_recv.at[src, slot],
            device_id={"node": to}, device_id_type=MESH,
        )

    def ret_copy(src, to, slot):
        return pltpu.make_async_remote_copy(
            src_ref=recv.at[src, to], dst_ref=ret.at[src, slot], send_sem=r_send.at[src, to], recv_sem=r_recv.at[src, slot],
            device_id={"node": to}, device_id_type=MESH,
        )

    def inc_copy(src, slot, chunk, plane):
        part = pl.ds(pl.multiple_of(chunk * rows, rows), rows)
        return pltpu.make_async_remote_copy(
            src_ref=inc.at[src, part], dst_ref=inc.at[slot, part], send_sem=i_send.at[src, chunk], recv_sem=i_recv.at[slot, chunk],
            device_id={"local": plane}, device_id_type=MESH,
        )

    for d in range(1, planes):
        meta_copy(l, other_plane(d)).start()

    def forward(src):
        @pl.when((src <= l) & (l < planes - 1))
        def _():
            block_copy(src, 0, l + 1).start()

        @pl.when((src >= l) & (l > 0))
        def _():
            block_copy(src, 1, l - 1).start()

    paired = jnp.minimum(l, planes - 1 - l)

    def source(j):
        near = (j + 1) // 2
        near = jnp.where(j % 2 == 1, l - near, l + near)
        far = j - paired
        far = jnp.where(l > planes - 1 - l, l - far, l + far)
        return jnp.where(j <= 2 * paired, near, far)

    def slot_codes():
        slot = lax.broadcasted_iota(jnp.int32, (slots, tok), 0)
        code = (slot // capacity) * (EPG * capacity) + (l // wsplit) * capacity + slot % capacity
        return code.astype(jnp.float32)

    def stage_pack(src):
        codes = slot_codes()
        selected = jnp.zeros((slots, tok), jnp.float32)
        for k in range(topk):
            selected = jnp.where(codes == metas[src, k : k + 1, :], 1.0, selected)
        selected = selected.astype(jnp.bfloat16)
        width = 512 if features % 512 == 0 else features

        @pl.loop(0, features // width)
        def _(c):
            cols = pl.ds(pl.multiple_of(c * width, width), width)
            part = jnp.dot(selected, gath[src, :, cols], preferred_element_type=jnp.float32)
            pack[src, :, :, cols] = part.astype(jnp.bfloat16).reshape(nodes, capacity, width)

        for d in range(1, nodes):
            pack_copy(src, other_node(d), n).start()
        recv[src, n] = pack[src, n]

    def stage_expert(src):
        for d in range(1, nodes):
            pack_copy(src, other_node(d), other_node(d)).wait_recv()
        width = 256 if ff % 256 == 0 else ff

        @pl.loop(0, ff // width)
        def _(c):
            cols = pl.ds(pl.multiple_of(c * width, width), width)
            x = recv[src].reshape(slots, features)
            gate = jnp.dot(x, wg[:, cols], preferred_element_type=jnp.float32)
            up = jnp.dot(x, wu[:, cols], preferred_element_type=jnp.float32)
            hid[:, cols] = (gate / (1.0 + jnp.exp(-gate)) * up).astype(jnp.bfloat16)

        wide = 512 if features % 512 == 0 else features

        @pl.loop(0, features // wide)
        def _(c):
            cols = pl.ds(pl.multiple_of(c * wide, wide), wide)
            part = jnp.dot(hid[...], wd[:, cols], preferred_element_type=jnp.float32)
            recv[src, :, :, cols] = part.astype(jnp.bfloat16).reshape(nodes, capacity, wide)

        for d in range(1, nodes):
            ret_copy(src, other_node(d), n).start()
        ret[src, n] = recv[src, n]

    def weights_of(src):
        codes = slot_codes()
        weight = jnp.zeros((slots, tok), jnp.float32)
        for k in range(topk):
            weight = jnp.where(codes == metas[src, k : k + 1, :], metas[src, topk + k : topk + k + 1, :], weight)
        return split_weight(weight.T)

    def wait_returned(src):
        for d in range(1, nodes):
            ret_copy(src, other_node(d), other_node(d)).wait_recv()

    def weighted(high, low, src, chunk):
        values = ret[src].reshape(slots, features)
        take = slice(chunk * rows, (chunk + 1) * rows)
        total = jnp.dot(high[take], values, preferred_element_type=jnp.float32)
        return total + jnp.dot(low[take], values, preferred_element_type=jnp.float32)

    def send_partial(src, chunk):
        @pl.when(src < l)
        def _():
            inc_copy(src, src, chunk, l - 1).start()

        @pl.when((src > l) & (src == l + 1))
        def _():
            inc_copy(src, planes, chunk, l + 1).start()

        @pl.when((src > l) & (src != l + 1))
        def _():
            inc_copy(src, src, chunk, l + 1).start()

    def stage_first(src):
        wait_returned(src)
        high, low = weights_of(src)
        for chunk in range(CHUNKS):
            inc[src, chunk * rows : (chunk + 1) * rows, :] = weighted(high, low, src, chunk).astype(jnp.bfloat16)
            send_partial(src, chunk)

    def stage_add(src):
        wait_returned(src)
        high, low = weights_of(src)
        for chunk in range(CHUNKS):
            total = weighted(high, low, src, chunk)
            inc_copy(src, src, chunk, other_plane(1)).wait_recv()
            part = slice(chunk * rows, (chunk + 1) * rows)
            inc[src, part, :] = (total + inc[src, part, :].astype(jnp.float32)).astype(jnp.bfloat16)
            send_partial(src, chunk)

    at_end = (l == 0) | (l == planes - 1)

    def step(j, carry):
        src = source(j)

        @pl.when(j > 0)
        def _():
            block_copy(src, 0, other_plane(1)).wait_recv()
            meta_copy(src, other_plane(1)).wait_recv()

        forward(src)
        stage_pack(src)

        @pl.when(j == 0)
        def _():
            for load in loads:
                load.wait()

        @pl.when((j > 1) & at_end)
        def _():
            stage_first(source(j - 1))

        stage_expert(src)
        return carry

    lax.fori_loop(0, planes, step, 0)

    @pl.when(at_end)
    def _():
        stage_first(source(planes - 1))

    @pl.when(jnp.logical_not(at_end))
    def _():
        def add(i, carry):
            stage_add(source(planes - 1 - i))
            return carry

        lax.fori_loop(0, planes - 1, add, 0)

    wait_returned(l)
    high, low = weights_of(l)
    for chunk in range(CHUNKS):
        part = slice(chunk * rows, (chunk + 1) * rows)

        @pl.when(l < planes - 1)
        def _():
            inc_copy(l, l, chunk, other_plane(1)).wait_recv()

        @pl.when(l > 0)
        def _():
            inc_copy(l, planes, chunk, other_plane(1)).wait_recv()

        right = jnp.where(l < planes - 1, inc[l, part, :].astype(jnp.float32), 0.0)
        left = jnp.where(l > 0, inc[planes, part, :].astype(jnp.float32), 0.0)
        out_ref[part, :] = (weighted(high, low, l, chunk) + right + left).astype(jnp.bfloat16)

    for d in range(1, planes):
        meta_copy(l, other_plane(d)).wait_send()

    def drain(src, carry):
        @pl.when((src <= l) & (l < planes - 1))
        def _():
            block_copy(src, 0, l + 1).wait_send()

        @pl.when((src >= l) & (l > 0))
        def _():
            block_copy(src, 1, l - 1).wait_send()

        for d in range(1, nodes):
            pack_copy(src, other_node(d), n).wait_send()
            ret_copy(src, other_node(d), n).wait_send()

        @pl.when(src != l)
        def _():
            for chunk in range(CHUNKS):
                inc_copy(src, src, chunk, other_plane(1)).wait_send()

        return carry

    lax.fori_loop(0, planes, drain, 0)


def on_device(tokens, expert_ids, gate_weights, gate_proj, up_proj, down_proj):
    tok_dev, features = tokens.shape
    topk = expert_ids.shape[1]
    ff = gate_proj.shape[2]
    nodes = lax.axis_size("node")
    planes = lax.axis_size("local")
    experts = EPG * nodes
    wsplit = planes // EPG
    capacity = 4 * tok_dev * topk // (3 * experts)
    codes = expert_ids * capacity + routing(expert_ids, experts)
    block = nodes * capacity * features * 2
    token_block = tok_dev * features * 2
    needed = planes * 3 * block + (2 * planes + 3) * token_block + 3 * features * ff * 2
    if needed > VMEM_BUDGET - 8 * 1024 * 1024 or planes < 2:
        return by_collectives(
            tokens, codes, gate_weights, gate_proj, up_proj, down_proj, experts, wsplit, capacity
        )
    meta_rows = -(-2 * topk // 8) * 8
    meta = jnp.concatenate(
        [codes.T.astype(jnp.float32), gate_weights.T, jnp.zeros((meta_rows - 2 * topk, tok_dev), jnp.float32)]
    )
    bf16 = jnp.bfloat16
    dma = pltpu.SemaphoreType.DMA
    vmem = pl.BlockSpec(memory_space=pltpu.VMEM)
    anywhere = pl.BlockSpec(memory_space=pl.ANY)
    return pl.pallas_call(
        functools.partial(kernel, nodes, planes, wsplit, capacity, topk),
        out_shape=jax.ShapeDtypeStruct((tok_dev, features), bf16),
        in_specs=[vmem, vmem, anywhere, anywhere, anywhere],
        out_specs=vmem,
        scratch_shapes=[
            pltpu.VMEM((planes, tok_dev, features), bf16),
            pltpu.VMEM((planes, meta_rows, tok_dev), jnp.float32),
            pltpu.VMEM((planes, nodes, capacity, features), bf16),
            pltpu.VMEM((planes, nodes, capacity, features), bf16),
            pltpu.VMEM((planes, nodes, capacity, features), bf16),
            pltpu.VMEM((planes + 1, tok_dev, features), bf16),
            pltpu.VMEM((nodes * capacity, ff), bf16),
            pltpu.VMEM((features, ff), bf16),
            pltpu.VMEM((features, ff), bf16),
            pltpu.VMEM((ff, features), bf16),
            dma((3,)),
            dma((2, planes)),
            dma((planes,)),
            dma((planes,)),
            dma((planes,)),
            dma((planes, nodes)),
            dma((planes, nodes)),
            dma((planes, nodes)),
            dma((planes, nodes)),
            dma((planes, CHUNKS)),
            dma((planes + 1, CHUNKS)),
        ],
        compiler_params=pltpu.CompilerParams(
            collective_id=0, has_side_effects=True, vmem_limit_bytes=VMEM_BUDGET
        ),
    )(tokens, meta, gate_proj, up_proj, down_proj)


def solution(mesh):
    return jax.shard_map(
        on_device,
        mesh=mesh,
        in_specs=(
            P(("parts", "node", "local"), None),
            P(("parts", "node", "local"), None),
            P(("parts", "node", "local"), None),
            P(("node", "local"), None, None),
            P(("node", "local"), None, None),
            P(("node", "local"), None, None),
        ),
        out_specs=P(("parts", "node", "local"), None),
        check_vma=False,
    )
```

```python
import functools

import jax
import jax.numpy as jnp
from jax import lax
from jax.experimental import pallas as pl
from jax.experimental.pallas import tpu as pltpu
from jax.sharding import PartitionSpec as P

EPG = 4
CHUNKS = 4
VMEM_BUDGET = 60 * 1024 * 1024
MESH = pl.DeviceIdType.MESH


def routing(expert_ids, experts):
    matches = expert_ids[:, :, None] == jnp.arange(experts, dtype=jnp.int32)[None, None, :]
    chosen = jnp.sum(matches.astype(jnp.int32), axis=1)
    ranking = jnp.cumsum(chosen, axis=0) - chosen
    rank = jnp.sum(jnp.where(matches, ranking[:, None, :], 0), axis=2)
    return rank


def split_weight(weight):
    high = weight.astype(jnp.bfloat16)
    low = (weight - high.astype(jnp.float32)).astype(jnp.bfloat16)
    return high, low


def expert_rows(received, gate_mat, up_mat, down_mat):
    features = received.shape[-1]
    flattened = received.reshape(-1, features)
    gate_act = jnp.dot(flattened, gate_mat, preferred_element_type=jnp.float32)
    up_act = jnp.dot(flattened, up_mat, preferred_element_type=jnp.float32)
    hidden = (jax.nn.silu(gate_act) * up_act).astype(jnp.bfloat16)
    output = jnp.dot(hidden, down_mat, preferred_element_type=jnp.float32).astype(jnp.bfloat16)
    return output.reshape(received.shape)


def by_collectives(tokens, codes, gate_weights, gate_proj, up_proj, down_proj, experts, wsplit, capacity):
    tok_dev, features = tokens.shape
    slots = jnp.arange(experts * capacity, dtype=jnp.int32)
    hit = codes[:, :, None] == slots[None, None, :]
    selected = jnp.any(hit, axis=1).astype(jnp.bfloat16).T
    packed = jnp.dot(selected, tokens, preferred_element_type=jnp.float32).astype(jnp.bfloat16)
    packed = jnp.broadcast_to(
        packed.reshape(experts, 1, capacity, features), (experts, wsplit, capacity, features)
    ).reshape(experts * wsplit, capacity, features)
    outputs = expert_rows(
        lax.all_to_all(packed, ("node", "local"), split_axis=0, concat_axis=0, tiled=True),
        gate_proj[0], up_proj[0], down_proj[0],
    )
    returned = lax.all_to_all(outputs, ("node", "local"), split_axis=0, concat_axis=0, tiled=True)
    weight = jnp.sum(jnp.where(hit, gate_weights[:, :, None], 0.0), axis=1)
    weight = jnp.broadcast_to(
        weight.reshape(tok_dev, experts, 1, capacity), (tok_dev, experts, wsplit, capacity)
    ).reshape(tok_dev, -1)
    high, low = split_weight(weight)
    returned = returned.reshape(-1, features)
    combined = jnp.dot(high, returned, preferred_element_type=jnp.float32)
    combined = combined + jnp.dot(low, returned, preferred_element_type=jnp.float32)
    return combined.astype(jnp.bfloat16)


def kernel(
    nodes, planes, wsplit, capacity, topk,
    tok_ref, meta_ref, gate_hbm, up_hbm, down_hbm, out_ref,
    gath, metas, sel, wts, pack, recv, ret, inc, gate_acc, up_acc, hid, wg, wu, wd,
    w_sem, g_send, g_recv, m_send, m_recv, p_send, p_recv, r_send, r_recv, i_send, i_recv,
):
    n = lax.axis_index("node")
    l = lax.axis_index("local")
    tok, features = tok_ref.shape
    slots = nodes * capacity
    width = features // CHUNKS
    f32, bf16 = jnp.float32, jnp.bfloat16

    def other_node(d):
        return lax.rem(n + d, nodes)

    def other_plane(d):
        return lax.rem(l + d, planes)

    def columns(c):
        return pl.ds(pl.multiple_of(c * width, width), width)

    barrier = pltpu.get_barrier_semaphore()
    for d in range(1, nodes):
        pl.semaphore_signal(barrier, inc=1, device_id={"node": other_node(d)}, device_id_type=MESH)
    for d in range(1, planes):
        pl.semaphore_signal(barrier, inc=1, device_id={"local": other_plane(d)}, device_id_type=MESH)

    metas[l] = meta_ref[...]
    for c in range(CHUNKS):
        gath[l, c] = tok_ref[:, c * width : (c + 1) * width]
    loads = [
        pltpu.make_async_copy(gate_hbm.at[0], wg, w_sem.at[0]),
        pltpu.make_async_copy(up_hbm.at[0], wu, w_sem.at[1]),
        pltpu.make_async_copy(down_hbm.at[0], wd, w_sem.at[2]),
    ]
    for load in loads:
        load.start()
    pl.semaphore_wait(barrier, nodes - 1 + planes - 1)

    def block_copy(src, c, way, plane):
        return pltpu.make_async_remote_copy(
            src_ref=gath.at[src, c], dst_ref=gath.at[src, c],
            send_sem=g_send.at[way, src, c], recv_sem=g_recv.at[src, c],
            device_id={"local": plane}, device_id_type=MESH,
        )

    def meta_copy(src, plane):
        return pltpu.make_async_remote_copy(
            src_ref=metas.at[src], dst_ref=metas.at[src], send_sem=m_send.at[plane], recv_sem=m_recv.at[src],
            device_id={"local": plane}, device_id_type=MESH,
        )

    def pack_copy(src, c, to, slot):
        return pltpu.make_async_remote_copy(
            src_ref=pack.at[src, c, to], dst_ref=recv.at[src, c, slot],
            send_sem=p_send.at[src, c, to], recv_sem=p_recv.at[src, c, slot],
            device_id={"node": to}, device_id_type=MESH,
        )

    def ret_copy(src, c, to, slot):
        return pltpu.make_async_remote_copy(
            src_ref=recv.at[src, c, to], dst_ref=ret.at[src, c, slot],
            send_sem=r_send.at[src, c, to], recv_sem=r_recv.at[src, c, slot],
            device_id={"node": to}, device_id_type=MESH,
        )

    def inc_copy(src, c, slot, plane):
        return pltpu.make_async_remote_copy(
            src_ref=inc.at[src, c], dst_ref=inc.at[slot, c],
            send_sem=i_send.at[src, c], recv_sem=i_recv.at[slot, c],
            device_id={"local": plane}, device_id_type=MESH,
        )

    def forward(src, c):
        @pl.when((src <= l) & (l < planes - 1))
        def _():
            block_copy(src, c, 0, l + 1).start()

        @pl.when((src >= l) & (l > 0))
        def _():
            block_copy(src, c, 1, l - 1).start()

    for d in range(1, planes):
        meta_copy(l, other_plane(d)).start()

    @pl.loop(0, CHUNKS)
    def _(c):
        forward(l, c)

    paired = jnp.minimum(l, planes - 1 - l)

    def source(j):
        near = (j + 1) // 2
        near = jnp.where(j % 2 == 1, l - near, l + near)
        far = j - paired
        far = jnp.where(l > planes - 1 - l, l - far, l + far)
        return jnp.where(j <= 2 * paired, near, far)

    def route(src):
        slot = lax.broadcasted_iota(jnp.int32, (slots, tok), 0)
        code = (slot // capacity) * (EPG * capacity) + (l // wsplit) * capacity + slot % capacity
        code = code.astype(f32)
        weight = jnp.zeros((slots, tok), f32)
        selected = jnp.zeros((slots, tok), f32)
        for k in range(topk):
            hit = code == metas[src, k : k + 1, :]
            selected = jnp.where(hit, 1.0, selected)
            weight = jnp.where(hit, metas[src, topk + k : topk + k + 1, :], weight)
        sel[src] = selected.astype(bf16)
        high, low = split_weight(weight.T)
        wts[src, 0] = high
        wts[src, 1] = low

    def stage_pack(src, c):
        part = jnp.dot(sel[src], gath[src, c], preferred_element_type=f32)
        pack[src, c] = part.astype(bf16).reshape(nodes, capacity, width)
        for d in range(1, nodes):
            pack_copy(src, c, other_node(d), n).start()
        recv[src, c, n] = pack[src, c, n]

    def stage_up(src, c):
        for d in range(1, nodes):
            pack_copy(src, c, other_node(d), other_node(d)).wait_recv()
        x = recv[src, c].reshape(slots, width)
        gate_acc[...] += jnp.dot(x, wg[columns(c), :], preferred_element_type=f32)
        up_acc[...] += jnp.dot(x, wu[columns(c), :], preferred_element_type=f32)

    def stage_down(src):
        gate = gate_acc[...]
        hid[...] = (gate / (1.0 + jnp.exp(-gate)) * up_acc[...]).astype(bf16)

        @pl.loop(0, CHUNKS)
        def _(c):
            part = jnp.dot(hid[...], wd[:, columns(c)], preferred_element_type=f32)
            recv[src, c] = part.astype(bf16).reshape(nodes, capacity, width)
            for d in range(1, nodes):
                ret_copy(src, c, other_node(d), n).start()
            ret[src, c, n] = recv[src, c, n]

    def weighted(src, c):
        for d in range(1, nodes):
            ret_copy(src, c, other_node(d), other_node(d)).wait_recv()
        both = jnp.dot(
            wts[src].reshape(2 * tok, slots), ret[src, c].reshape(slots, width), preferred_element_type=f32
        )
        return both[:tok] + both[tok:]

    def send_partial(src, c):
        @pl.when(src < l)
        def _():
            inc_copy(src, c, src, l - 1).start()

        @pl.when(src == l + 1)
        def _():
            inc_copy(src, c, planes, l + 1).start()

        @pl.when(src > l + 1)
        def _():
            inc_copy(src, c, src, l + 1).start()

    def stage_first(src, c):
        inc[src, c] = weighted(src, c).astype(bf16)
        send_partial(src, c)

    def stage_add(src, c):
        total = weighted(src, c)
        inc_copy(src, c, src, other_plane(1)).wait_recv()
        inc[src, c] = (total + inc[src, c].astype(f32)).astype(bf16)
        send_partial(src, c)

    at_end = (l == 0) | (l == planes - 1)

    def step(j, carry):
        src = source(j)

        @pl.when(j > 0)
        def _():
            meta_copy(src, other_plane(1)).wait_recv()

        route(src)
        gate_acc[...] = jnp.zeros_like(gate_acc)
        up_acc[...] = jnp.zeros_like(up_acc)

        @pl.loop(0, CHUNKS)
        def _(c):
            @pl.when(j > 0)
            def _():
                block_copy(src, c, 0, other_plane(1)).wait_recv()
                forward(src, c)

            stage_pack(src, c)

            @pl.when((j > 1) & at_end)
            def _():
                stage_first(source(j - 1), c)

            @pl.when((j == 0) & (c == 1))
            def _():
                loads[0].wait()
                loads[1].wait()

            @pl.when(c > 0)
            def _():
                stage_up(src, c - 1)

        stage_up(src, CHUNKS - 1)

        @pl.when(j == 0)
        def _():
            loads[2].wait()

        stage_down(src)
        return carry

    lax.fori_loop(0, planes, step, 0)

    @pl.when(at_end)
    def _():
        @pl.loop(0, CHUNKS)
        def _(c):
            stage_first(source(planes - 1), c)

    nearer_right = l > planes - 1 - l
    toward = jnp.where(nearer_right, 1, -1)
    count = jnp.maximum(l, planes - 1 - l)

    @pl.when(jnp.logical_not(at_end))
    def _():
        def add(i, carry):
            late = i - (count - (planes - 1 - count))

            @pl.loop(0, CHUNKS)
            def _(c):
                stage_add(l - toward * (i + 1), c)

                @pl.when(late >= 0)
                def _():
                    stage_add(l + toward * (late + 1), c)

            return carry

        lax.fori_loop(0, count, add, 0)

    @pl.loop(0, CHUNKS)
    def _(c):
        total = weighted(l, c)

        @pl.when(l < planes - 1)
        def _():
            inc_copy(l, c, l, other_plane(1)).wait_recv()

        @pl.when(l > 0)
        def _():
            inc_copy(l, c, planes, other_plane(1)).wait_recv()

        right = jnp.where(l < planes - 1, inc[l, c].astype(f32), 0.0)
        left = jnp.where(l > 0, inc[planes, c].astype(f32), 0.0)
        out_ref[:, columns(c)] = (total + right + left).astype(bf16)

    for d in range(1, planes):
        meta_copy(l, other_plane(d)).wait_send()

    def drain(src, carry):
        @pl.loop(0, CHUNKS)
        def _(c):
            @pl.when((src <= l) & (l < planes - 1))
            def _():
                block_copy(src, c, 0, l + 1).wait_send()

            @pl.when((src >= l) & (l > 0))
            def _():
                block_copy(src, c, 1, l - 1).wait_send()

            for d in range(1, nodes):
                pack_copy(src, c, other_node(d), n).wait_send()
                ret_copy(src, c, other_node(d), n).wait_send()

            @pl.when(src != l)
            def _():
                inc_copy(src, c, src, other_plane(1)).wait_send()

        return carry

    lax.fori_loop(0, planes, drain, 0)


def on_device(tokens, expert_ids, gate_weights, gate_proj, up_proj, down_proj):
    tok_dev, features = tokens.shape
    topk = expert_ids.shape[1]
    ff = gate_proj.shape[2]
    nodes = lax.axis_size("node")
    planes = lax.axis_size("local")
    experts = EPG * nodes
    wsplit = planes // EPG
    capacity = 4 * tok_dev * topk // (3 * experts)
    codes = expert_ids * capacity + routing(expert_ids, experts)
    block = nodes * capacity * features * 2
    token_block = tok_dev * features * 2
    needed = planes * 3 * block + (2 * planes + 3) * token_block + 3 * features * ff * 2
    if needed > VMEM_BUDGET - 8 * 1024 * 1024 or planes != EPG or features % CHUNKS:
        return by_collectives(
            tokens, codes, gate_weights, gate_proj, up_proj, down_proj, experts, wsplit, capacity
        )
    meta_rows = -(-2 * topk // 8) * 8
    meta = jnp.concatenate(
        [codes.T.astype(jnp.float32), gate_weights.T, jnp.zeros((meta_rows - 2 * topk, tok_dev), jnp.float32)]
    )
    width = features // CHUNKS
    bf16 = jnp.bfloat16
    dma = pltpu.SemaphoreType.DMA
    vmem = pl.BlockSpec(memory_space=pltpu.VMEM)
    anywhere = pl.BlockSpec(memory_space=pl.ANY)
    return pl.pallas_call(
        functools.partial(kernel, nodes, planes, wsplit, capacity, topk),
        out_shape=jax.ShapeDtypeStruct((tok_dev, features), bf16),
        in_specs=[vmem, vmem, anywhere, anywhere, anywhere],
        out_specs=vmem,
        scratch_shapes=[
            pltpu.VMEM((planes, CHUNKS, tok_dev, width), bf16),
            pltpu.VMEM((planes, meta_rows, tok_dev), jnp.float32),
            pltpu.VMEM((planes, nodes * capacity, tok_dev), bf16),
            pltpu.VMEM((planes, 2, tok_dev, nodes * capacity), bf16),
            pltpu.VMEM((planes, CHUNKS, nodes, capacity, width), bf16),
            pltpu.VMEM((planes, CHUNKS, nodes, capacity, width), bf16),
            pltpu.VMEM((planes, CHUNKS, nodes, capacity, width), bf16),
            pltpu.VMEM((planes + 1, CHUNKS, tok_dev, width), bf16),
            pltpu.VMEM((nodes * capacity, ff), jnp.float32),
            pltpu.VMEM((nodes * capacity, ff), jnp.float32),
            pltpu.VMEM((nodes * capacity, ff), bf16),
            pltpu.VMEM((features, ff), bf16),
            pltpu.VMEM((features, ff), bf16),
            pltpu.VMEM((ff, features), bf16),
            dma((3,)),
            dma((2, planes, CHUNKS)),
            dma((planes, CHUNKS)),
            dma((planes,)),
            dma((planes,)),
            dma((planes, CHUNKS, nodes)),
            dma((planes, CHUNKS, nodes)),
            dma((planes, CHUNKS, nodes)),
            dma((planes, CHUNKS, nodes)),
            dma((planes, CHUNKS)),
            dma((planes + 1, CHUNKS)),
        ],
        compiler_params=pltpu.CompilerParams(
            collective_id=0, has_side_effects=True, vmem_limit_bytes=VMEM_BUDGET
        ),
    )(tokens, meta, gate_proj, up_proj, down_proj)


def solution(mesh):
    return jax.shard_map(
        on_device,
        mesh=mesh,
        in_specs=(
            P(("parts", "node", "local"), None),
            P(("parts", "node", "local"), None),
            P(("parts", "node", "local"), None),
            P(("node", "local"), None, None),
            P(("node", "local"), None, None),
            P(("node", "local"), None, None),
        ),
        out_specs=P(("parts", "node", "local"), None),
        check_vma=False,
    )
```

```python
import functools

import jax
import jax.numpy as jnp
from jax import lax
from jax.experimental import pallas as pl
from jax.experimental.pallas import tpu as pltpu
from jax.sharding import PartitionSpec as P

EPG = 4
CHUNKS = 4
VMEM_BUDGET = 60 * 1024 * 1024
MESH = pl.DeviceIdType.MESH


def routing(expert_ids, experts):
    matches = expert_ids[:, :, None] == jnp.arange(experts, dtype=jnp.int32)[None, None, :]
    chosen = jnp.sum(matches.astype(jnp.int32), axis=1)
    ranking = jnp.cumsum(chosen, axis=0) - chosen
    rank = jnp.sum(jnp.where(matches, ranking[:, None, :], 0), axis=2)
    return rank


def split_weight(weight):
    high = weight.astype(jnp.bfloat16)
    low = (weight - high.astype(jnp.float32)).astype(jnp.bfloat16)
    return high, low


def expert_rows(received, gate_mat, up_mat, down_mat):
    features = received.shape[-1]
    flattened = received.reshape(-1, features)
    gate_act = jnp.dot(flattened, gate_mat, preferred_element_type=jnp.float32)
    up_act = jnp.dot(flattened, up_mat, preferred_element_type=jnp.float32)
    hidden = (jax.nn.silu(gate_act) * up_act).astype(jnp.bfloat16)
    output = jnp.dot(hidden, down_mat, preferred_element_type=jnp.float32).astype(jnp.bfloat16)
    return output.reshape(received.shape)


def by_collectives(tokens, codes, gate_weights, gate_proj, up_proj, down_proj, experts, wsplit, capacity):
    tok_dev, features = tokens.shape
    slots = jnp.arange(experts * capacity, dtype=jnp.int32)
    hit = codes[:, :, None] == slots[None, None, :]
    selected = jnp.any(hit, axis=1).astype(jnp.bfloat16).T
    packed = jnp.dot(selected, tokens, preferred_element_type=jnp.float32).astype(jnp.bfloat16)
    packed = jnp.broadcast_to(
        packed.reshape(experts, 1, capacity, features), (experts, wsplit, capacity, features)
    ).reshape(experts * wsplit, capacity, features)
    outputs = expert_rows(
        lax.all_to_all(packed, ("node", "local"), split_axis=0, concat_axis=0, tiled=True),
        gate_proj[0], up_proj[0], down_proj[0],
    )
    returned = lax.all_to_all(outputs, ("node", "local"), split_axis=0, concat_axis=0, tiled=True)
    weight = jnp.sum(jnp.where(hit, gate_weights[:, :, None], 0.0), axis=1)
    weight = jnp.broadcast_to(
        weight.reshape(tok_dev, experts, 1, capacity), (tok_dev, experts, wsplit, capacity)
    ).reshape(tok_dev, -1)
    high, low = split_weight(weight)
    returned = returned.reshape(-1, features)
    combined = jnp.dot(high, returned, preferred_element_type=jnp.float32)
    combined = combined + jnp.dot(low, returned, preferred_element_type=jnp.float32)
    return combined.astype(jnp.bfloat16)


def kernel(
    nodes, planes, wsplit, capacity, topk,
    tok_ref, meta_ref, gate_hbm, up_hbm, down_hbm, out_ref,
    gath, metas, sel, wts, pack, recv, ret, inc, gate_acc, up_acc, hid, wg, wu, wd,
    w_sem, g_send, g_recv, m_send, m_recv, p_send, p_recv, r_send, r_recv, i_send, i_recv,
):
    n = lax.axis_index("node")
    l = lax.axis_index("local")
    tok, features = tok_ref.shape
    slots = nodes * capacity
    width = features // CHUNKS
    f32, bf16 = jnp.float32, jnp.bfloat16

    def other_node(d):
        return lax.rem(n + d, nodes)

    def other_plane(d):
        return lax.rem(l + d, planes)

    def columns(c):
        return pl.ds(pl.multiple_of(c * width, width), width)

    barrier = pltpu.get_barrier_semaphore()
    for d in range(1, nodes):
        pl.semaphore_signal(barrier, inc=1, device_id={"node": other_node(d)}, device_id_type=MESH)
    for d in range(1, planes):
        pl.semaphore_signal(barrier, inc=1, device_id={"local": other_plane(d)}, device_id_type=MESH)

    metas[l] = meta_ref[...]
    for c in range(CHUNKS):
        gath[l, c] = tok_ref[:, c * width : (c + 1) * width]
    loads = [
        pltpu.make_async_copy(gate_hbm.at[0], wg, w_sem.at[0]),
        pltpu.make_async_copy(up_hbm.at[0], wu, w_sem.at[1]),
        pltpu.make_async_copy(down_hbm.at[0], wd, w_sem.at[2]),
    ]
    for load in loads:
        load.start()
    pl.semaphore_wait(barrier, nodes - 1 + planes - 1)

    def block_copy(src, c, way, plane):
        return pltpu.make_async_remote_copy(
            src_ref=gath.at[src, c], dst_ref=gath.at[src, c],
            send_sem=g_send.at[way, src, c], recv_sem=g_recv.at[src, c],
            device_id={"local": plane}, device_id_type=MESH,
        )

    def meta_copy(src, plane):
        return pltpu.make_async_remote_copy(
            src_ref=metas.at[src], dst_ref=metas.at[src], send_sem=m_send.at[plane], recv_sem=m_recv.at[src],
            device_id={"local": plane}, device_id_type=MESH,
        )

    def pack_copy(src, c, to, slot):
        return pltpu.make_async_remote_copy(
            src_ref=pack.at[src, c, to], dst_ref=recv.at[src, c, slot],
            send_sem=p_send.at[src, c, to], recv_sem=p_recv.at[src, c, slot],
            device_id={"node": to}, device_id_type=MESH,
        )

    def ret_copy(src, c, to, slot):
        return pltpu.make_async_remote_copy(
            src_ref=recv.at[src, c, to], dst_ref=ret.at[src, c, slot],
            send_sem=r_send.at[src, c, to], recv_sem=r_recv.at[src, c, slot],
            device_id={"node": to}, device_id_type=MESH,
        )

    def inc_copy(src, c, slot, plane):
        return pltpu.make_async_remote_copy(
            src_ref=inc.at[src, c], dst_ref=inc.at[slot, c],
            send_sem=i_send.at[src, c], recv_sem=i_recv.at[slot, c],
            device_id={"local": plane}, device_id_type=MESH,
        )

    def forward(src, c):
        @pl.when((src <= l) & (l < planes - 1))
        def _():
            block_copy(src, c, 0, l + 1).start()

        @pl.when((src >= l) & (l > 0))
        def _():
            block_copy(src, c, 1, l - 1).start()

    for d in range(1, planes):
        meta_copy(l, other_plane(d)).start()

    @pl.loop(0, CHUNKS)
    def _(c):
        forward(l, c)

    paired = jnp.minimum(l, planes - 1 - l)

    def source(j):
        near = (j + 1) // 2
        near = jnp.where(j % 2 == 1, l - near, l + near)
        far = j - paired
        far = jnp.where(l > planes - 1 - l, l - far, l + far)
        return jnp.where(j <= 2 * paired, near, far)

    def route(src):
        slot = lax.broadcasted_iota(jnp.int32, (slots, tok), 0)
        code = (slot // capacity) * (EPG * capacity) + (l // wsplit) * capacity + slot % capacity
        code = code.astype(f32)
        weight = jnp.zeros((slots, tok), f32)
        selected = jnp.zeros((slots, tok), f32)
        for k in range(topk):
            hit = code == metas[src, k : k + 1, :]
            selected = jnp.where(hit, 1.0, selected)
            weight = jnp.where(hit, metas[src, topk + k : topk + k + 1, :], weight)
        sel[src] = selected.astype(bf16)
        high, low = split_weight(weight.T)
        wts[src, 0] = high
        wts[src, 1] = low

    def stage_pack(src, c):
        part = jnp.dot(sel[src], gath[src, c], preferred_element_type=f32)
        pack[src, c] = part.astype(bf16).reshape(nodes, capacity, width)
        for d in range(1, nodes):
            pack_copy(src, c, other_node(d), n).start()
        recv[src, c, n] = pack[src, c, n]

    def stage_up(src, c):
        for d in range(1, nodes):
            pack_copy(src, c, other_node(d), other_node(d)).wait_recv()
        x = recv[src, c].reshape(slots, width)
        gate_acc[...] += jnp.dot(x, wg[columns(c), :], preferred_element_type=f32)
        up_acc[...] += jnp.dot(x, wu[columns(c), :], preferred_element_type=f32)

    def stage_down(src):
        gate = gate_acc[...]
        hid[...] = (gate / (1.0 + jnp.exp(-gate)) * up_acc[...]).astype(bf16)

        @pl.loop(0, CHUNKS)
        def _(c):
            part = jnp.dot(hid[...], wd[:, columns(c)], preferred_element_type=f32)
            recv[src, c] = part.astype(bf16).reshape(nodes, capacity, width)
            for d in range(1, nodes):
                ret_copy(src, c, other_node(d), n).start()
            ret[src, c, n] = recv[src, c, n]

    def weighted(src, c):
        for d in range(1, nodes):
            ret_copy(src, c, other_node(d), other_node(d)).wait_recv()
        both = jnp.dot(
            wts[src].reshape(2 * tok, slots), ret[src, c].reshape(slots, width), preferred_element_type=f32
        )
        return both[:tok] + both[tok:]

    def send_partial(src, c):
        @pl.when(src < l)
        def _():
            inc_copy(src, c, src, l - 1).start()

        @pl.when(src == l + 1)
        def _():
            inc_copy(src, c, planes, l + 1).start()

        @pl.when(src > l + 1)
        def _():
            inc_copy(src, c, src, l + 1).start()

    def stage_first(src, c):
        inc[src, c] = weighted(src, c).astype(bf16)
        send_partial(src, c)

    def stage_add(src, c):
        total = weighted(src, c)
        inc_copy(src, c, src, other_plane(1)).wait_recv()
        inc[src, c] = (total + inc[src, c].astype(f32)).astype(bf16)
        send_partial(src, c)

    at_end = (l == 0) | (l == planes - 1)

    def stage_route(j):
        src = source(j)

        @pl.when(j > 0)
        def _():
            meta_copy(src, other_plane(1)).wait_recv()

        route(src)

    def stage_arrive(j, c):
        src = source(j)

        @pl.when(j > 0)
        def _():
            block_copy(src, c, 0, other_plane(1)).wait_recv()
            forward(src, c)

        stage_pack(src, c)

    def wait_first_weights(j, c):
        @pl.when((j == 0) & (c == 0))
        def _():
            loads[0].wait()
            loads[1].wait()

    middle = jnp.logical_not(at_end)

    @pl.when(middle)
    def _():
        stage_route(0)

        @pl.loop(0, CHUNKS)
        def _(c):
            stage_arrive(0, c)

    def step(j, carry):
        src = source(j)
        even = j % 2 == 0
        next_one = middle & (j + 1 < planes) & (even | (j + 1 > 2 * paired))
        next_two = middle & even & (j + 2 <= 2 * paired)

        @pl.when(next_one)
        def _():
            stage_route(j + 1)

        @pl.when(next_two)
        def _():
            stage_route(j + 2)

        @pl.when(at_end)
        def _():
            stage_route(j)

        gate_acc[...] = jnp.zeros_like(gate_acc)
        up_acc[...] = jnp.zeros_like(up_acc)

        @pl.loop(0, CHUNKS + 1)
        def _(c):
            @pl.when(at_end & (c < CHUNKS))
            def _():
                stage_arrive(j, c)

                @pl.when(j > 1)
                def _():
                    stage_first(source(j - 1), c)

            @pl.when(next_one & (c < CHUNKS))
            def _():
                stage_arrive(j + 1, c)

            @pl.when(next_two & (c < CHUNKS))
            def _():
                stage_arrive(j + 2, c)

            @pl.when(c > 0)
            def _():
                wait_first_weights(j, c - 1)
                stage_up(src, c - 1)

        @pl.when(j == 0)
        def _():
            loads[2].wait()

        stage_down(src)
        return carry

    lax.fori_loop(0, planes, step, 0)

    @pl.when(at_end)
    def _():
        @pl.loop(0, CHUNKS)
        def _(c):
            stage_first(source(planes - 1), c)

    nearer_right = l > planes - 1 - l
    toward = jnp.where(nearer_right, 1, -1)
    count = jnp.maximum(l, planes - 1 - l)

    @pl.when(middle)
    def _():
        def add(i, carry):
            late = i - (count - (planes - 1 - count))

            @pl.loop(0, CHUNKS)
            def _(c):
                stage_add(l - toward * (i + 1), c)

                @pl.when(late >= 0)
                def _():
                    stage_add(l + toward * (late + 1), c)

            return carry

        lax.fori_loop(0, count, add, 0)

    @pl.loop(0, CHUNKS)
    def _(c):
        total = weighted(l, c)

        @pl.when(l < planes - 1)
        def _():
            inc_copy(l, c, l, other_plane(1)).wait_recv()

        @pl.when(l > 0)
        def _():
            inc_copy(l, c, planes, other_plane(1)).wait_recv()

        right = jnp.where(l < planes - 1, inc[l, c].astype(f32), 0.0)
        left = jnp.where(l > 0, inc[planes, c].astype(f32), 0.0)
        out_ref[:, columns(c)] = (total + right + left).astype(bf16)

    for d in range(1, planes):
        meta_copy(l, other_plane(d)).wait_send()

    def drain(src, carry):
        @pl.loop(0, CHUNKS)
        def _(c):
            @pl.when((src <= l) & (l < planes - 1))
            def _():
                block_copy(src, c, 0, l + 1).wait_send()

            @pl.when((src >= l) & (l > 0))
            def _():
                block_copy(src, c, 1, l - 1).wait_send()

            for d in range(1, nodes):
                pack_copy(src, c, other_node(d), n).wait_send()
                ret_copy(src, c, other_node(d), n).wait_send()

            @pl.when(src != l)
            def _():
                inc_copy(src, c, src, other_plane(1)).wait_send()

        return carry

    lax.fori_loop(0, planes, drain, 0)


def on_device(tokens, expert_ids, gate_weights, gate_proj, up_proj, down_proj):
    tok_dev, features = tokens.shape
    topk = expert_ids.shape[1]
    ff = gate_proj.shape[2]
    nodes = lax.axis_size("node")
    planes = lax.axis_size("local")
    experts = EPG * nodes
    wsplit = planes // EPG
    capacity = 4 * tok_dev * topk // (3 * experts)
    codes = expert_ids * capacity + routing(expert_ids, experts)
    block = nodes * capacity * features * 2
    token_block = tok_dev * features * 2
    needed = planes * 3 * block + (2 * planes + 3) * token_block + 3 * features * ff * 2
    if needed > VMEM_BUDGET - 8 * 1024 * 1024 or planes != EPG or features % CHUNKS:
        return by_collectives(
            tokens, codes, gate_weights, gate_proj, up_proj, down_proj, experts, wsplit, capacity
        )
    meta_rows = -(-2 * topk // 8) * 8
    meta = jnp.concatenate(
        [codes.T.astype(jnp.float32), gate_weights.T, jnp.zeros((meta_rows - 2 * topk, tok_dev), jnp.float32)]
    )
    width = features // CHUNKS
    bf16 = jnp.bfloat16
    dma = pltpu.SemaphoreType.DMA
    vmem = pl.BlockSpec(memory_space=pltpu.VMEM)
    anywhere = pl.BlockSpec(memory_space=pl.ANY)
    return pl.pallas_call(
        functools.partial(kernel, nodes, planes, wsplit, capacity, topk),
        out_shape=jax.ShapeDtypeStruct((tok_dev, features), bf16),
        in_specs=[vmem, vmem, anywhere, anywhere, anywhere],
        out_specs=vmem,
        scratch_shapes=[
            pltpu.VMEM((planes, CHUNKS, tok_dev, width), bf16),
            pltpu.VMEM((planes, meta_rows, tok_dev), jnp.float32),
            pltpu.VMEM((planes, nodes * capacity, tok_dev), bf16),
            pltpu.VMEM((planes, 2, tok_dev, nodes * capacity), bf16),
            pltpu.VMEM((planes, CHUNKS, nodes, capacity, width), bf16),
            pltpu.VMEM((planes, CHUNKS, nodes, capacity, width), bf16),
            pltpu.VMEM((planes, CHUNKS, nodes, capacity, width), bf16),
            pltpu.VMEM((planes + 1, CHUNKS, tok_dev, width), bf16),
            pltpu.VMEM((nodes * capacity, ff), jnp.float32),
            pltpu.VMEM((nodes * capacity, ff), jnp.float32),
            pltpu.VMEM((nodes * capacity, ff), bf16),
            pltpu.VMEM((features, ff), bf16),
            pltpu.VMEM((features, ff), bf16),
            pltpu.VMEM((ff, features), bf16),
            dma((3,)),
            dma((2, planes, CHUNKS)),
            dma((planes, CHUNKS)),
            dma((planes,)),
            dma((planes,)),
            dma((planes, CHUNKS, nodes)),
            dma((planes, CHUNKS, nodes)),
            dma((planes, CHUNKS, nodes)),
            dma((planes, CHUNKS, nodes)),
            dma((planes, CHUNKS)),
            dma((planes + 1, CHUNKS)),
        ],
        compiler_params=pltpu.CompilerParams(
            collective_id=0, has_side_effects=True, vmem_limit_bytes=VMEM_BUDGET
        ),
    )(tokens, meta, gate_proj, up_proj, down_proj)


def solution(mesh):
    return jax.shard_map(
        on_device,
        mesh=mesh,
        in_specs=(
            P(("parts", "node", "local"), None),
            P(("parts", "node", "local"), None),
            P(("parts", "node", "local"), None),
            P(("node", "local"), None, None),
            P(("node", "local"), None, None),
            P(("node", "local"), None, None),
        ),
        out_specs=P(("parts", "node", "local"), None),
        check_vma=False,
    )
```

```python
import functools

import jax
import jax.numpy as jnp
from jax import lax
from jax.experimental import pallas as pl
from jax.experimental.pallas import tpu as pltpu
from jax.sharding import PartitionSpec as P

EPG = 4
CHUNKS = 7
VMEM_BUDGET = 60 * 1024 * 1024
MESH = pl.DeviceIdType.MESH


def routing(expert_ids, experts):
    matches = expert_ids[:, :, None] == jnp.arange(experts, dtype=jnp.int32)[None, None, :]
    chosen = jnp.sum(matches.astype(jnp.int32), axis=1)
    ranking = jnp.cumsum(chosen, axis=0) - chosen
    rank = jnp.sum(jnp.where(matches, ranking[:, None, :], 0), axis=2)
    return rank


def split_weight(weight):
    high = weight.astype(jnp.bfloat16)
    low = (weight - high.astype(jnp.float32)).astype(jnp.bfloat16)
    return high, low


def expert_rows(received, gate_mat, up_mat, down_mat):
    features = received.shape[-1]
    flattened = received.reshape(-1, features)
    gate_act = jnp.dot(flattened, gate_mat, preferred_element_type=jnp.float32)
    up_act = jnp.dot(flattened, up_mat, preferred_element_type=jnp.float32)
    hidden = (jax.nn.silu(gate_act) * up_act).astype(jnp.bfloat16)
    output = jnp.dot(hidden, down_mat, preferred_element_type=jnp.float32).astype(jnp.bfloat16)
    return output.reshape(received.shape)


def by_collectives(tokens, codes, gate_weights, gate_proj, up_proj, down_proj, experts, wsplit, capacity):
    tok_dev, features = tokens.shape
    slots = jnp.arange(experts * capacity, dtype=jnp.int32)
    hit = codes[:, :, None] == slots[None, None, :]
    selected = jnp.any(hit, axis=1).astype(jnp.bfloat16).T
    packed = jnp.dot(selected, tokens, preferred_element_type=jnp.float32).astype(jnp.bfloat16)
    packed = jnp.broadcast_to(
        packed.reshape(experts, 1, capacity, features), (experts, wsplit, capacity, features)
    ).reshape(experts * wsplit, capacity, features)
    outputs = expert_rows(
        lax.all_to_all(packed, ("node", "local"), split_axis=0, concat_axis=0, tiled=True),
        gate_proj[0], up_proj[0], down_proj[0],
    )
    returned = lax.all_to_all(outputs, ("node", "local"), split_axis=0, concat_axis=0, tiled=True)
    weight = jnp.sum(jnp.where(hit, gate_weights[:, :, None], 0.0), axis=1)
    weight = jnp.broadcast_to(
        weight.reshape(tok_dev, experts, 1, capacity), (tok_dev, experts, wsplit, capacity)
    ).reshape(tok_dev, -1)
    high, low = split_weight(weight)
    returned = returned.reshape(-1, features)
    combined = jnp.dot(high, returned, preferred_element_type=jnp.float32)
    combined = combined + jnp.dot(low, returned, preferred_element_type=jnp.float32)
    return combined.astype(jnp.bfloat16)


def kernel(
    nodes, planes, wsplit, capacity, topk,
    tok_ref, meta_ref, gate_hbm, up_hbm, down_hbm, out_ref,
    gath, metas, sel, wts, pack, recv, ret, inc, gate_acc, up_acc, hid, wg, wu, wd,
    w_sem, g_send, g_recv, m_send, m_recv, p_send, p_recv, r_send, r_recv, i_send, i_recv,
):
    n = lax.axis_index("node")
    l = lax.axis_index("local")
    tok, features = tok_ref.shape
    slots = nodes * capacity
    width = features // CHUNKS
    f32, bf16 = jnp.float32, jnp.bfloat16

    def other_node(d):
        return lax.rem(n + d, nodes)

    def other_plane(d):
        return lax.rem(l + d, planes)

    def columns(c):
        return pl.ds(pl.multiple_of(c * width, width), width)

    barrier = pltpu.get_barrier_semaphore()
    for d in range(1, nodes):
        pl.semaphore_signal(barrier, inc=1, device_id={"node": other_node(d)}, device_id_type=MESH)
    for d in range(1, planes):
        pl.semaphore_signal(barrier, inc=1, device_id={"local": other_plane(d)}, device_id_type=MESH)

    for c in range(CHUNKS):
        gath[l, c] = tok_ref[:, c * width : (c + 1) * width]
    loads = [
        pltpu.make_async_copy(gate_hbm.at[0], wg, w_sem.at[0]),
        pltpu.make_async_copy(up_hbm.at[0], wu, w_sem.at[1]),
        pltpu.make_async_copy(down_hbm.at[0], wd, w_sem.at[2]),
    ]
    for load in loads:
        load.start()
    pl.semaphore_wait(barrier, nodes - 1 + planes - 1)

    def block_copy(src, c, way, plane):
        return pltpu.make_async_remote_copy(
            src_ref=gath.at[src, c], dst_ref=gath.at[src, c],
            send_sem=g_send.at[way, src, c], recv_sem=g_recv.at[src, c],
            device_id={"local": plane}, device_id_type=MESH,
        )

    def meta_copy(src, plane):
        return pltpu.make_async_remote_copy(
            src_ref=metas.at[src], dst_ref=metas.at[src], send_sem=m_send.at[plane], recv_sem=m_recv.at[src],
            device_id={"local": plane}, device_id_type=MESH,
        )

    def pack_copy(src, c, to, slot):
        return pltpu.make_async_remote_copy(
            src_ref=pack.at[src, c, to], dst_ref=recv.at[src, c, slot],
            send_sem=p_send.at[src, c, to], recv_sem=p_recv.at[src, c, slot],
            device_id={"node": to}, device_id_type=MESH,
        )

    def ret_copy(src, c, to, slot):
        return pltpu.make_async_remote_copy(
            src_ref=recv.at[src, c, to], dst_ref=ret.at[src, c, slot],
            send_sem=r_send.at[src, c, to], recv_sem=r_recv.at[src, c, slot],
            device_id={"node": to}, device_id_type=MESH,
        )

    def inc_copy(src, c, slot, plane):
        return pltpu.make_async_remote_copy(
            src_ref=inc.at[src, c], dst_ref=inc.at[slot, c],
            send_sem=i_send.at[src, c], recv_sem=i_recv.at[slot, c],
            device_id={"local": plane}, device_id_type=MESH,
        )

    def forward(src, c):
        @pl.when((src <= l) & (l < planes - 1))
        def _():
            block_copy(src, c, 0, l + 1).start()

        @pl.when((src >= l) & (l > 0))
        def _():
            block_copy(src, c, 1, l - 1).start()

    @pl.loop(0, CHUNKS)
    def _(c):
        forward(l, c)

    experts = EPG * nodes
    row = lax.broadcasted_iota(jnp.int32, (experts, tok), 0).astype(f32)
    chosen = jnp.zeros((experts, tok), f32)
    for k in range(topk):
        chosen = jnp.where(row == meta_ref[k : k + 1, :], 1.0, chosen)
    earlier = lax.broadcasted_iota(jnp.int32, (tok, tok), 0) < lax.broadcasted_iota(jnp.int32, (tok, tok), 1)
    ranks = jnp.dot(chosen.astype(bf16), jnp.where(earlier, 1.0, 0.0).astype(bf16), preferred_element_type=f32)
    code_of = row * capacity + ranks
    metas[l] = meta_ref[...]
    for k in range(topk):
        picked = jnp.where(row == meta_ref[k : k + 1, :], code_of, 0.0)
        metas[l, k : k + 1, :] = jnp.sum(picked, axis=0, keepdims=True)
    for d in range(1, planes):
        meta_copy(l, other_plane(d)).start()

    paired = jnp.minimum(l, planes - 1 - l)

    def source(j):
        near = (j + 1) // 2
        near = jnp.where(j % 2 == 1, l - near, l + near)
        far = j - paired
        far = jnp.where(l > planes - 1 - l, l - far, l + far)
        return jnp.where(j <= 2 * paired, near, far)

    def route(src):
        slot = lax.broadcasted_iota(jnp.int32, (slots, tok), 0)
        code = (slot // capacity) * (EPG * capacity) + (l // wsplit) * capacity + slot % capacity
        code = code.astype(f32)
        weight = jnp.zeros((slots, tok), f32)
        selected = jnp.zeros((slots, tok), f32)
        for k in range(topk):
            hit = code == metas[src, k : k + 1, :]
            selected = jnp.where(hit, 1.0, selected)
            weight = jnp.where(hit, metas[src, topk + k : topk + k + 1, :], weight)
        sel[src] = selected.astype(bf16)
        high, low = split_weight(weight.T)
        wts[src, 0] = high
        wts[src, 1] = low

    def stage_pack(src, c):
        part = jnp.dot(sel[src], gath[src, c], preferred_element_type=f32)
        pack[src, c] = part.astype(bf16).reshape(nodes, capacity, width)
        for d in range(1, nodes):
            pack_copy(src, c, other_node(d), n).start()
        recv[src, c, n] = pack[src, c, n]

    def stage_up(src, c):
        for d in range(1, nodes):
            pack_copy(src, c, other_node(d), other_node(d)).wait_recv()
        x = recv[src, c].reshape(slots, width)
        gate_acc[...] += jnp.dot(x, wg[columns(c), :], preferred_element_type=f32)
        up_acc[...] += jnp.dot(x, wu[columns(c), :], preferred_element_type=f32)

    def stage_down(src):
        gate = gate_acc[...]
        hid[...] = (gate / (1.0 + jnp.exp(-gate)) * up_acc[...]).astype(bf16)

        @pl.loop(0, CHUNKS)
        def _(c):
            part = jnp.dot(hid[...], wd[:, columns(c)], preferred_element_type=f32)
            recv[src, c] = part.astype(bf16).reshape(nodes, capacity, width)
            for d in range(1, nodes):
                ret_copy(src, c, other_node(d), n).start()
            ret[src, c, n] = recv[src, c, n]

    def weighted(src, c):
        for d in range(1, nodes):
            ret_copy(src, c, other_node(d), other_node(d)).wait_recv()
        both = jnp.dot(
            wts[src].reshape(2 * tok, slots), ret[src, c].reshape(slots, width), preferred_element_type=f32
        )
        return both[:tok] + both[tok:]

    def send_partial(src, c):
        @pl.when(src < l)
        def _():
            inc_copy(src, c, src, l - 1).start()

        @pl.when(src == l + 1)
        def _():
            inc_copy(src, c, planes, l + 1).start()

        @pl.when(src > l + 1)
        def _():
            inc_copy(src, c, src, l + 1).start()

    def stage_first(src, c):
        inc[src, c] = weighted(src, c).astype(bf16)
        send_partial(src, c)

    def stage_add(src, c):
        total = weighted(src, c)
        inc_copy(src, c, src, other_plane(1)).wait_recv()
        inc[src, c] = (total + inc[src, c].astype(f32)).astype(bf16)
        send_partial(src, c)

    at_end = (l == 0) | (l == planes - 1)

    def stage_route(j):
        src = source(j)

        @pl.when(j > 0)
        def _():
            meta_copy(src, other_plane(1)).wait_recv()

        route(src)

    def stage_arrive(j, c):
        src = source(j)

        @pl.when(j > 0)
        def _():
            block_copy(src, c, 0, other_plane(1)).wait_recv()
            forward(src, c)

        stage_pack(src, c)

    def wait_first_weights(j, c):
        @pl.when((j == 0) & (c == 0))
        def _():
            loads[0].wait()
            loads[1].wait()

    middle = jnp.logical_not(at_end)

    @pl.when(middle)
    def _():
        stage_route(0)

        @pl.loop(0, CHUNKS)
        def _(c):
            stage_arrive(0, c)

    def step(j, carry):
        src = source(j)
        even = j % 2 == 0
        next_one = middle & (j + 1 < planes) & (even | (j + 1 > 2 * paired))
        next_two = middle & even & (j + 2 <= 2 * paired)

        @pl.when(next_one)
        def _():
            stage_route(j + 1)

        @pl.when(next_two)
        def _():
            stage_route(j + 2)

        @pl.when(at_end)
        def _():
            stage_route(j)

        gate_acc[...] = jnp.zeros_like(gate_acc)
        up_acc[...] = jnp.zeros_like(up_acc)

        @pl.loop(0, CHUNKS + 1)
        def _(c):
            @pl.when(at_end & (c < CHUNKS))
            def _():
                stage_arrive(j, c)

            @pl.when(next_one & (c < CHUNKS))
            def _():
                stage_arrive(j + 1, c)

            @pl.when(next_two & (c < CHUNKS))
            def _():
                stage_arrive(j + 2, c)

            @pl.when(c > 0)
            def _():
                wait_first_weights(j, c - 1)
                stage_up(src, c - 1)

            @pl.when(at_end & (c < CHUNKS) & (j > 1))
            def _():
                stage_first(source(j - 1), c)

        @pl.when(j == 0)
        def _():
            loads[2].wait()

        stage_down(src)
        return carry

    lax.fori_loop(0, planes, step, 0)

    @pl.when(at_end)
    def _():
        @pl.loop(0, CHUNKS)
        def _(c):
            stage_first(source(planes - 1), c)

    nearer_right = l > planes - 1 - l
    toward = jnp.where(nearer_right, 1, -1)
    count = jnp.maximum(l, planes - 1 - l)

    @pl.when(middle)
    def _():
        def add(i, carry):
            late = i - (count - (planes - 1 - count))

            @pl.loop(0, CHUNKS)
            def _(c):
                stage_add(l - toward * (i + 1), c)

                @pl.when(late >= 0)
                def _():
                    stage_add(l + toward * (late + 1), c)

            return carry

        lax.fori_loop(0, count, add, 0)

    @pl.loop(0, CHUNKS)
    def _(c):
        total = weighted(l, c)

        @pl.when(l < planes - 1)
        def _():
            inc_copy(l, c, l, other_plane(1)).wait_recv()

        @pl.when(l > 0)
        def _():
            inc_copy(l, c, planes, other_plane(1)).wait_recv()

        right = jnp.where(l < planes - 1, inc[l, c].astype(f32), 0.0)
        left = jnp.where(l > 0, inc[planes, c].astype(f32), 0.0)
        out_ref[:, columns(c)] = (total + right + left).astype(bf16)

    for d in range(1, planes):
        meta_copy(l, other_plane(d)).wait_send()

    def drain(src, carry):
        @pl.loop(0, CHUNKS)
        def _(c):
            @pl.when((src <= l) & (l < planes - 1))
            def _():
                block_copy(src, c, 0, l + 1).wait_send()

            @pl.when((src >= l) & (l > 0))
            def _():
                block_copy(src, c, 1, l - 1).wait_send()

            for d in range(1, nodes):
                pack_copy(src, c, other_node(d), n).wait_send()
                ret_copy(src, c, other_node(d), n).wait_send()

            @pl.when(src != l)
            def _():
                inc_copy(src, c, src, other_plane(1)).wait_send()

        return carry

    lax.fori_loop(0, planes, drain, 0)


def on_device(tokens, expert_ids, gate_weights, gate_proj, up_proj, down_proj):
    tok_dev, features = tokens.shape
    topk = expert_ids.shape[1]
    ff = gate_proj.shape[2]
    nodes = lax.axis_size("node")
    planes = lax.axis_size("local")
    experts = EPG * nodes
    wsplit = planes // EPG
    capacity = 4 * tok_dev * topk // (3 * experts)
    block = nodes * capacity * features * 2
    token_block = tok_dev * features * 2
    needed = planes * 3 * block + (2 * planes + 3) * token_block + 3 * features * ff * 2
    if needed > VMEM_BUDGET - 8 * 1024 * 1024 or planes != EPG or features % CHUNKS:
        codes = expert_ids * capacity + routing(expert_ids, experts)
        return by_collectives(
            tokens, codes, gate_weights, gate_proj, up_proj, down_proj, experts, wsplit, capacity
        )
    meta_rows = -(-2 * topk // 8) * 8
    meta = jnp.concatenate(
        [expert_ids.T.astype(jnp.float32), gate_weights.T, jnp.zeros((meta_rows - 2 * topk, tok_dev), jnp.float32)]
    )
    width = features // CHUNKS
    bf16 = jnp.bfloat16
    dma = pltpu.SemaphoreType.DMA
    vmem = pl.BlockSpec(memory_space=pltpu.VMEM)
    anywhere = pl.BlockSpec(memory_space=pl.ANY)
    return pl.pallas_call(
        functools.partial(kernel, nodes, planes, wsplit, capacity, topk),
        out_shape=jax.ShapeDtypeStruct((tok_dev, features), bf16),
        in_specs=[vmem, vmem, anywhere, anywhere, anywhere],
        out_specs=vmem,
        scratch_shapes=[
            pltpu.VMEM((planes, CHUNKS, tok_dev, width), bf16),
            pltpu.VMEM((planes, meta_rows, tok_dev), jnp.float32),
            pltpu.VMEM((planes, nodes * capacity, tok_dev), bf16),
            pltpu.VMEM((planes, 2, tok_dev, nodes * capacity), bf16),
            pltpu.VMEM((planes, CHUNKS, nodes, capacity, width), bf16),
            pltpu.VMEM((planes, CHUNKS, nodes, capacity, width), bf16),
            pltpu.VMEM((planes, CHUNKS, nodes, capacity, width), bf16),
            pltpu.VMEM((planes + 1, CHUNKS, tok_dev, width), bf16),
            pltpu.VMEM((nodes * capacity, ff), jnp.float32),
            pltpu.VMEM((nodes * capacity, ff), jnp.float32),
            pltpu.VMEM((nodes * capacity, ff), bf16),
            pltpu.VMEM((features, ff), bf16),
            pltpu.VMEM((features, ff), bf16),
            pltpu.VMEM((ff, features), bf16),
            dma((3,)),
            dma((2, planes, CHUNKS)),
            dma((planes, CHUNKS)),
            dma((planes,)),
            dma((planes,)),
            dma((planes, CHUNKS, nodes)),
            dma((planes, CHUNKS, nodes)),
            dma((planes, CHUNKS, nodes)),
            dma((planes, CHUNKS, nodes)),
            dma((planes, CHUNKS)),
            dma((planes + 1, CHUNKS)),
        ],
        compiler_params=pltpu.CompilerParams(
            collective_id=0, has_side_effects=True, vmem_limit_bytes=VMEM_BUDGET
        ),
    )(tokens, meta, gate_proj, up_proj, down_proj)


def solution(mesh):
    return jax.shard_map(
        on_device,
        mesh=mesh,
        in_specs=(
            P(("parts", "node", "local"), None),
            P(("parts", "node", "local"), None),
            P(("parts", "node", "local"), None),
            P(("node", "local"), None, None),
            P(("node", "local"), None, None),
            P(("node", "local"), None, None),
        ),
        out_specs=P(("parts", "node", "local"), None),
        check_vma=False,
    )
```

```python
import functools

import jax
import jax.numpy as jnp
from jax import lax
from jax.experimental import pallas as pl
from jax.experimental.pallas import tpu as pltpu
from jax.sharding import PartitionSpec as P

EPG = 4
CHUNKS = 4
HALVES = 2
PER = CHUNKS // HALVES
VMEM_BUDGET = 60 * 1024 * 1024
MESH = pl.DeviceIdType.MESH


def routing(expert_ids, experts):
    matches = expert_ids[:, :, None] == jnp.arange(experts, dtype=jnp.int32)[None, None, :]
    chosen = jnp.sum(matches.astype(jnp.int32), axis=1)
    ranking = jnp.cumsum(chosen, axis=0) - chosen
    rank = jnp.sum(jnp.where(matches, ranking[:, None, :], 0), axis=2)
    return rank


def split_weight(weight):
    high = weight.astype(jnp.bfloat16)
    low = (weight - high.astype(jnp.float32)).astype(jnp.bfloat16)
    return high, low


def expert_rows(received, gate_mat, up_mat, down_mat):
    features = received.shape[-1]
    flattened = received.reshape(-1, features)
    gate_act = jnp.dot(flattened, gate_mat, preferred_element_type=jnp.float32)
    up_act = jnp.dot(flattened, up_mat, preferred_element_type=jnp.float32)
    hidden = (jax.nn.silu(gate_act) * up_act).astype(jnp.bfloat16)
    output = jnp.dot(hidden, down_mat, preferred_element_type=jnp.float32).astype(jnp.bfloat16)
    return output.reshape(received.shape)


def by_collectives(tokens, codes, gate_weights, gate_proj, up_proj, down_proj, experts, wsplit, capacity):
    tok_dev, features = tokens.shape
    slots = jnp.arange(experts * capacity, dtype=jnp.int32)
    hit = codes[:, :, None] == slots[None, None, :]
    selected = jnp.any(hit, axis=1).astype(jnp.bfloat16).T
    packed = jnp.dot(selected, tokens, preferred_element_type=jnp.float32).astype(jnp.bfloat16)
    packed = jnp.broadcast_to(
        packed.reshape(experts, 1, capacity, features), (experts, wsplit, capacity, features)
    ).reshape(experts * wsplit, capacity, features)
    outputs = expert_rows(
        lax.all_to_all(packed, ("node", "local"), split_axis=0, concat_axis=0, tiled=True),
        gate_proj[0], up_proj[0], down_proj[0],
    )
    returned = lax.all_to_all(outputs, ("node", "local"), split_axis=0, concat_axis=0, tiled=True)
    weight = jnp.sum(jnp.where(hit, gate_weights[:, :, None], 0.0), axis=1)
    weight = jnp.broadcast_to(
        weight.reshape(tok_dev, experts, 1, capacity), (tok_dev, experts, wsplit, capacity)
    ).reshape(tok_dev, -1)
    high, low = split_weight(weight)
    returned = returned.reshape(-1, features)
    combined = jnp.dot(high, returned, preferred_element_type=jnp.float32)
    combined = combined + jnp.dot(low, returned, preferred_element_type=jnp.float32)
    return combined.astype(jnp.bfloat16)


def kernel(
    nodes, planes, wsplit, capacity, topk,
    tok_ref, meta_ref, gate_hbm, up_hbm, down_hbm, out_ref,
    gath, metas, sel, wts, pack, recv, ret, inc, gate_acc, up_acc, hid, wg, wu, wd,
    w_sem, g_send, g_recv, m_send, m_recv, p_send, p_recv, r_send, r_recv, i_send, i_recv,
):
    n = lax.axis_index("node")
    l = lax.axis_index("local")
    tok, features = tok_ref.shape
    slots = nodes * capacity
    width = features // CHUNKS
    wide = features // HALVES
    f32, bf16 = jnp.float32, jnp.bfloat16

    def other_node(d):
        return lax.rem(n + d, nodes)

    def other_plane(d):
        return lax.rem(l + d, planes)

    def within(c):
        return pl.ds(pl.multiple_of((c % PER) * width, width), width)

    def halves(h):
        return pl.ds(pl.multiple_of(h * wide, wide), wide)

    def columns(c):
        return pl.ds(pl.multiple_of(c * width, width), width)

    barrier = pltpu.get_barrier_semaphore()
    for d in range(1, nodes):
        pl.semaphore_signal(barrier, inc=1, device_id={"node": other_node(d)}, device_id_type=MESH)
    for d in range(1, planes):
        pl.semaphore_signal(barrier, inc=1, device_id={"local": other_plane(d)}, device_id_type=MESH)

    for c in range(CHUNKS):
        gath[l, c] = tok_ref[:, c * width : (c + 1) * width]
    loads = [
        pltpu.make_async_copy(gate_hbm.at[0], wg, w_sem.at[0]),
        pltpu.make_async_copy(up_hbm.at[0], wu, w_sem.at[1]),
        pltpu.make_async_copy(down_hbm.at[0], wd, w_sem.at[2]),
    ]
    for load in loads:
        load.start()
    pl.semaphore_wait(barrier, nodes - 1 + planes - 1)

    def block_copy(src, c, way, plane):
        return pltpu.make_async_remote_copy(
            src_ref=gath.at[src, c], dst_ref=gath.at[src, c],
            send_sem=g_send.at[way, src, c], recv_sem=g_recv.at[src, c],
            device_id={"local": plane}, device_id_type=MESH,
        )

    def meta_copy(src, plane):
        return pltpu.make_async_remote_copy(
            src_ref=metas.at[src], dst_ref=metas.at[src], send_sem=m_send.at[plane], recv_sem=m_recv.at[src],
            device_id={"local": plane}, device_id_type=MESH,
        )

    def pack_copy(src, c, to, slot):
        return pltpu.make_async_remote_copy(
            src_ref=pack.at[src, c, to], dst_ref=recv.at[src, c, slot],
            send_sem=p_send.at[src, c, to], recv_sem=p_recv.at[src, c, slot],
            device_id={"node": to}, device_id_type=MESH,
        )

    def ret_copy(src, c, to, slot):
        return pltpu.make_async_remote_copy(
            src_ref=recv.at[src, c, to], dst_ref=ret.at[src, c, slot],
            send_sem=r_send.at[src, c, to], recv_sem=r_recv.at[src, c, slot],
            device_id={"node": to}, device_id_type=MESH,
        )

    def inc_copy(src, c, slot, plane):
        return pltpu.make_async_remote_copy(
            src_ref=inc.at[src, c], dst_ref=inc.at[slot, c],
            send_sem=i_send.at[src, c], recv_sem=i_recv.at[slot, c],
            device_id={"local": plane}, device_id_type=MESH,
        )

    def forward(src, c):
        @pl.when((src <= l) & (l < planes - 1))
        def _():
            block_copy(src, c, 0, l + 1).start()

        @pl.when((src >= l) & (l > 0))
        def _():
            block_copy(src, c, 1, l - 1).start()

    @pl.loop(0, CHUNKS)
    def _(c):
        forward(l, c)

    experts = EPG * nodes
    row = lax.broadcasted_iota(jnp.int32, (experts, tok), 0).astype(f32)
    chosen = jnp.zeros((experts, tok), f32)
    for k in range(topk):
        chosen = jnp.where(row == meta_ref[k : k + 1, :], 1.0, chosen)
    earlier = lax.broadcasted_iota(jnp.int32, (tok, tok), 0) < lax.broadcasted_iota(jnp.int32, (tok, tok), 1)
    ranks = jnp.dot(chosen.astype(bf16), jnp.where(earlier, 1.0, 0.0).astype(bf16), preferred_element_type=f32)
    code_of = row * capacity + ranks
    metas[l] = meta_ref[...]
    for k in range(topk):
        picked = jnp.where(row == meta_ref[k : k + 1, :], code_of, 0.0)
        metas[l, k : k + 1, :] = jnp.sum(picked, axis=0, keepdims=True)
    for d in range(1, planes):
        meta_copy(l, other_plane(d)).start()

    paired = jnp.minimum(l, planes - 1 - l)

    def source(j):
        near = (j + 1) // 2
        near = jnp.where(j % 2 == 1, l - near, l + near)
        far = j - paired
        far = jnp.where(l > planes - 1 - l, l - far, l + far)
        return jnp.where(j <= 2 * paired, near, far)

    def route(src):
        slot = lax.broadcasted_iota(jnp.int32, (slots, tok), 0)
        code = (slot // capacity) * (EPG * capacity) + (l // wsplit) * capacity + slot % capacity
        code = code.astype(f32)
        weight = jnp.zeros((slots, tok), f32)
        selected = jnp.zeros((slots, tok), f32)
        for k in range(topk):
            hit = code == metas[src, k : k + 1, :]
            selected = jnp.where(hit, 1.0, selected)
            weight = jnp.where(hit, metas[src, topk + k : topk + k + 1, :], weight)
        sel[src] = selected.astype(bf16)
        high, low = split_weight(weight.T)
        wts[src, 0] = high
        wts[src, 1] = low

    def stage_pack(src, c):
        part = jnp.dot(sel[src], gath[src, c], preferred_element_type=f32)
        h = c // PER
        pack[src, h, :, :, within(c)] = part.astype(bf16).reshape(nodes, capacity, width)

        @pl.when(c % PER == PER - 1)
        def _():
            for d in range(1, nodes):
                pack_copy(src, h, other_node(d), n).start()
            recv[src, h, n] = pack[src, h, n]

    def stage_up(src, h):
        for d in range(1, nodes):
            pack_copy(src, h, other_node(d), other_node(d)).wait_recv()
        x = recv[src, h].reshape(slots, wide)
        gate_acc[...] += jnp.dot(x, wg[halves(h), :], preferred_element_type=f32)
        up_acc[...] += jnp.dot(x, wu[halves(h), :], preferred_element_type=f32)

    def stage_down(src):
        gate = gate_acc[...]
        hid[...] = (gate / (1.0 + jnp.exp(-gate)) * up_acc[...]).astype(bf16)

        @pl.loop(0, HALVES)
        def _(h):
            for q in range(PER):
                part = jnp.dot(hid[...], wd[:, columns(h * PER + q)], preferred_element_type=f32)
                recv[src, h, :, :, q * width : (q + 1) * width] = part.astype(bf16).reshape(nodes, capacity, width)
            for d in range(1, nodes):
                ret_copy(src, h, other_node(d), n).start()
            ret[src, h, n] = recv[src, h, n]

    def weighted(src, c):
        h = c // PER

        @pl.when(c % PER == 0)
        def _():
            for d in range(1, nodes):
                ret_copy(src, h, other_node(d), other_node(d)).wait_recv()

        values = ret[src, h, :, :, within(c)].reshape(slots, width)
        both = jnp.dot(wts[src].reshape(2 * tok, slots), values, preferred_element_type=f32)
        return both[:tok] + both[tok:]

    def send_partial(src, c):
        @pl.when(src < l)
        def _():
            inc_copy(src, c, src, l - 1).start()

        @pl.when(src == l + 1)
        def _():
            inc_copy(src, c, planes, l + 1).start()

        @pl.when(src > l + 1)
        def _():
            inc_copy(src, c, src, l + 1).start()

    def stage_first(src, c):
        inc[src, c] = weighted(src, c).astype(bf16)
        send_partial(src, c)

    def stage_add(src, c):
        total = weighted(src, c)
        inc_copy(src, c, src, other_plane(1)).wait_recv()
        inc[src, c] = (total + inc[src, c].astype(f32)).astype(bf16)
        send_partial(src, c)

    at_end = (l == 0) | (l == planes - 1)

    def stage_route(j):
        src = source(j)

        @pl.when(j > 0)
        def _():
            meta_copy(src, other_plane(1)).wait_recv()

        route(src)

    def stage_arrive(j, c):
        src = source(j)

        @pl.when(j > 0)
        def _():
            block_copy(src, c, 0, other_plane(1)).wait_recv()
            forward(src, c)

        stage_pack(src, c)

    def wait_first_weights(j, c):
        @pl.when((j == 0) & (c == 0))
        def _():
            loads[0].wait()
            loads[1].wait()

    middle = jnp.logical_not(at_end)

    @pl.when(middle)
    def _():
        stage_route(0)

        @pl.loop(0, CHUNKS)
        def _(c):
            stage_arrive(0, c)

    def step(j, carry):
        src = source(j)
        even = j % 2 == 0
        next_one = middle & (j + 1 < planes) & (even | (j + 1 > 2 * paired))
        next_two = middle & even & (j + 2 <= 2 * paired)

        @pl.when(next_one)
        def _():
            stage_route(j + 1)

        @pl.when(next_two)
        def _():
            stage_route(j + 2)

        @pl.when(at_end)
        def _():
            stage_route(j)

        gate_acc[...] = jnp.zeros_like(gate_acc)
        up_acc[...] = jnp.zeros_like(up_acc)

        @pl.loop(0, CHUNKS + 1)
        def _(c):
            @pl.when(at_end & (c < CHUNKS))
            def _():
                stage_arrive(j, c)

            @pl.when(next_one & (c < CHUNKS))
            def _():
                stage_arrive(j + 1, c)

            @pl.when(next_two & (c < CHUNKS))
            def _():
                stage_arrive(j + 2, c)

            @pl.when(at_end & (c < CHUNKS) & (j > 1))
            def _():
                stage_first(source(j - 1), c)

            @pl.when((c > 0) & (c % PER == 0))
            def _():
                wait_first_weights(j, c // PER - 1)
                stage_up(src, c // PER - 1)

        @pl.when(j == 0)
        def _():
            loads[2].wait()

        stage_down(src)
        return carry

    lax.fori_loop(0, planes, step, 0)

    @pl.when(at_end)
    def _():
        @pl.loop(0, CHUNKS)
        def _(c):
            stage_first(source(planes - 1), c)

    nearer_right = l > planes - 1 - l
    toward = jnp.where(nearer_right, 1, -1)
    count = jnp.maximum(l, planes - 1 - l)

    @pl.when(middle)
    def _():
        def add(i, carry):
            late = i - (count - (planes - 1 - count))

            @pl.loop(0, CHUNKS)
            def _(c):
                stage_add(l - toward * (i + 1), c)

                @pl.when(late >= 0)
                def _():
                    stage_add(l + toward * (late + 1), c)

            return carry

        lax.fori_loop(0, count, add, 0)

    @pl.loop(0, CHUNKS)
    def _(c):
        total = weighted(l, c)

        @pl.when(l < planes - 1)
        def _():
            inc_copy(l, c, l, other_plane(1)).wait_recv()

        @pl.when(l > 0)
        def _():
            inc_copy(l, c, planes, other_plane(1)).wait_recv()

        right = jnp.where(l < planes - 1, inc[l, c].astype(f32), 0.0)
        left = jnp.where(l > 0, inc[planes, c].astype(f32), 0.0)
        out_ref[:, columns(c)] = (total + right + left).astype(bf16)

    for d in range(1, planes):
        meta_copy(l, other_plane(d)).wait_send()

    def drain(src, carry):
        @pl.loop(0, CHUNKS)
        def _(c):
            @pl.when((src <= l) & (l < planes - 1))
            def _():
                block_copy(src, c, 0, l + 1).wait_send()

            @pl.when((src >= l) & (l > 0))
            def _():
                block_copy(src, c, 1, l - 1).wait_send()

            @pl.when(c < HALVES)
            def _():
                for d in range(1, nodes):
                    pack_copy(src, c, other_node(d), n).wait_send()
                    ret_copy(src, c, other_node(d), n).wait_send()

            @pl.when(src != l)
            def _():
                inc_copy(src, c, src, other_plane(1)).wait_send()

        return carry

    lax.fori_loop(0, planes, drain, 0)


def on_device(tokens, expert_ids, gate_weights, gate_proj, up_proj, down_proj):
    tok_dev, features = tokens.shape
    topk = expert_ids.shape[1]
    ff = gate_proj.shape[2]
    nodes = lax.axis_size("node")
    planes = lax.axis_size("local")
    experts = EPG * nodes
    wsplit = planes // EPG
    capacity = 4 * tok_dev * topk // (3 * experts)
    block = nodes * capacity * features * 2
    token_block = tok_dev * features * 2
    needed = planes * 3 * block + (2 * planes + 3) * token_block + 3 * features * ff * 2
    if needed > VMEM_BUDGET - 8 * 1024 * 1024 or planes != EPG or features % CHUNKS:
        codes = expert_ids * capacity + routing(expert_ids, experts)
        return by_collectives(
            tokens, codes, gate_weights, gate_proj, up_proj, down_proj, experts, wsplit, capacity
        )
    meta_rows = -(-2 * topk // 8) * 8
    meta = jnp.concatenate(
        [expert_ids.T.astype(jnp.float32), gate_weights.T, jnp.zeros((meta_rows - 2 * topk, tok_dev), jnp.float32)]
    )
    width, wide = features // CHUNKS, features // HALVES
    bf16 = jnp.bfloat16
    dma = pltpu.SemaphoreType.DMA
    vmem = pl.BlockSpec(memory_space=pltpu.VMEM)
    anywhere = pl.BlockSpec(memory_space=pl.ANY)
    return pl.pallas_call(
        functools.partial(kernel, nodes, planes, wsplit, capacity, topk),
        out_shape=jax.ShapeDtypeStruct((tok_dev, features), bf16),
        in_specs=[vmem, vmem, anywhere, anywhere, anywhere],
        out_specs=vmem,
        scratch_shapes=[
            pltpu.VMEM((planes, CHUNKS, tok_dev, width), bf16),
            pltpu.VMEM((planes, meta_rows, tok_dev), jnp.float32),
            pltpu.VMEM((planes, nodes * capacity, tok_dev), bf16),
            pltpu.VMEM((planes, 2, tok_dev, nodes * capacity), bf16),
            pltpu.VMEM((planes, HALVES, nodes, capacity, wide), bf16),
            pltpu.VMEM((planes, HALVES, nodes, capacity, wide), bf16),
            pltpu.VMEM((planes, HALVES, nodes, capacity, wide), bf16),
            pltpu.VMEM((planes + 1, CHUNKS, tok_dev, width), bf16),
            pltpu.VMEM((nodes * capacity, ff), jnp.float32),
            pltpu.VMEM((nodes * capacity, ff), jnp.float32),
            pltpu.VMEM((nodes * capacity, ff), bf16),
            pltpu.VMEM((features, ff), bf16),
            pltpu.VMEM((features, ff), bf16),
            pltpu.VMEM((ff, features), bf16),
            dma((3,)),
            dma((2, planes, CHUNKS)),
            dma((planes, CHUNKS)),
            dma((planes,)),
            dma((planes,)),
            dma((planes, HALVES, nodes)),
            dma((planes, HALVES, nodes)),
            dma((planes, HALVES, nodes)),
            dma((planes, HALVES, nodes)),
            dma((planes, CHUNKS)),
            dma((planes + 1, CHUNKS)),
        ],
        compiler_params=pltpu.CompilerParams(
            collective_id=0, has_side_effects=True, vmem_limit_bytes=VMEM_BUDGET
        ),
    )(tokens, meta, gate_proj, up_proj, down_proj)


def solution(mesh):
    return jax.shard_map(
        on_device,
        mesh=mesh,
        in_specs=(
            P(("parts", "node", "local"), None),
            P(("parts", "node", "local"), None),
            P(("parts", "node", "local"), None),
            P(("node", "local"), None, None),
            P(("node", "local"), None, None),
            P(("node", "local"), None, None),
        ),
        out_specs=P(("parts", "node", "local"), None),
        check_vma=False,
    )
```
